32 devices in a mesh: diag: 16 (over z, y, x), off: 2 (over core).
Axes of the slice: x: 2, y: 2, z: 4, core: 2. Of those that a mesh axis runs over, the one named last changes fastest.
Arguments:
- trunk: bfloat16 [16, 1, 64, 128], P('diag'), may hold values from -6 to 6
- w_first: bfloat16 [48, 128, 3, 3], replicated, may hold values from -0.1875 to 0.1875
- b_first: float32 [48], replicated, may hold values from -3 to 3
- w_second: bfloat16 [48, 48, 3, 3], replicated, may hold values from -0.3125 to 0.3125
- b_second: float32 [48], replicated, may hold values from -3 to 3
Outputs:
- contact_tiles: bfloat16 [16, 2, 1, 48, 128, 128], P('diag', 'off')
The draws below stay inside these ranges and needn't reach their ends.
All inputs are finite; a program needn't handle non-finite values.
Results may differ from the reference program's by a relative error of at most 0.0043.
Values may be sent and summed in bfloat16 or wider, within the bound.
A program may use at most 128 MiB of HBM per device.

```python
import jax
import jax.numpy as jnp
from jax import lax

W = 128
C = 64
HID = 48
B = 1
NP = 16
BAND = 2
NB = 2048


def steps_of(key, dims, pieces, low, largest):
    def one(axis_at, parts):
        heights = jax.random.uniform(jax.random.fold_in(jax.random.fold_in(key, 6), axis_at), (parts,), jnp.float32, low / len(pieces), largest / len(pieces))
        return jnp.repeat(jnp.exp(heights), dims[axis_at] // parts).reshape((-1,) + (1,) * (len(dims) - axis_at - 1))

    loudness = one(*pieces[0])
    for cut in pieces[1:]:
        loudness = loudness * one(*cut)
    return loudness


def normal_values(key, dims, scale, reach, split=(), kind=jnp.bfloat16):
    gain = steps_of(key, dims, split, -0.22, 0.18) if split else 1.0
    entries = jax.random.normal(key, dims, jnp.float32) * scale * gain
    return jnp.minimum(jnp.maximum(entries, -reach), reach).astype(kind)


def setup_inputs(seed: int = 0) -> dict:
    splits = jax.random.split(jax.random.key(seed), 6)
    return {
        "trunk": normal_values(splits[0], (NP, B, C, W), 1.0, 6.0, ((0, 16),)),
        "w_first": normal_values(splits[1], (HID, 2 * C, 3, 3), (18 * C) ** -0.5, 0.1875),
        "b_first": normal_values(splits[2], (HID,), 0.5, 3.0, (), jnp.float32),
        "w_second": normal_values(splits[3], (HID, HID, 3, 3), (9 * HID) ** -0.5, 0.3125),
        "b_second": normal_values(splits[4], (HID,), 0.5, 3.0, (), jnp.float32),
    }


def band_mask(row_tile, col_tile, start, extent):
    offsets = start + jnp.arange(extent, dtype=jnp.int32)
    row_bins = row_tile * W + offsets
    col_bins = col_tile * W + offsets
    row_ok = (row_bins >= 0) & (row_bins < NB)
    col_ok = (col_bins >= 0) & (col_bins < NB)
    gap = jnp.floor_divide(col_bins, W)[None, :] - jnp.floor_divide(row_bins, W)[:, None]
    return row_ok[:, None] & col_ok[None, :] & (gap >= 0) & (gap < BAND)


def dilated(inputs, weights, rate):
    return lax.conv_general_dilated(inputs, weights, (1, 1), "VALID", rhs_dilation=(rate, rate),
                                    dimension_numbers=("NCHW", "OIHW", "NCHW"),
                                    precision=lax.Precision.HIGHEST)


def reference(trunk, w_first, b_first, w_second, b_second):
    flat = jnp.transpose(trunk.astype(jnp.float32), (1, 2, 0, 3)).reshape(B, C, NB)
    padded = jnp.pad(flat, ((0, 0), (0, 0), (6, 6 + BAND * W)))
    first = w_first.astype(jnp.float32)
    second = w_second.astype(jnp.float32)
    extent = W + 12

    def one_tile(index):
        row_tile = (index // BAND).astype(jnp.int32)
        col_tile = (row_tile + index % BAND).astype(jnp.int32)
        rows = lax.dynamic_slice(padded, (jnp.int32(0), jnp.int32(0), row_tile * W), (B, C, extent))
        cols = lax.dynamic_slice(padded, (jnp.int32(0), jnp.int32(0), col_tile * W), (B, C, extent))
        features = jnp.concatenate([jnp.broadcast_to(rows[:, :, :, None], (B, C, extent, extent)),
                                    jnp.broadcast_to(cols[:, :, None, :], (B, C, extent, extent))], axis=1)
        features = jnp.where(band_mask(row_tile, col_tile, -6, extent)[None, None], features, 0.0)
        pre = dilated(features, first, 2) + b_first[None, :, None, None]
        hidden = jnp.where(band_mask(row_tile, col_tile, -4, extent - 4)[None, None],
                           jnp.maximum(pre, 0.0), 0.0)
        hidden = hidden.astype(jnp.bfloat16).astype(jnp.float32)
        result = dilated(hidden, second, 4) + b_second[None, :, None, None]
        return result.astype(jnp.bfloat16)

    tiles = lax.map(one_tile, jnp.arange(NP * BAND, dtype=jnp.int32))
    return tiles.reshape(NP, BAND, B, HID, W, W)
```

```python
import functools

import jax
import jax.numpy as jnp
from jax import lax
from jax.experimental import pallas as pl
from jax.experimental.pallas import tpu as pltpu
from jax.sharding import PartitionSpec as P

MESH = pl.DeviceIdType.MESH
TAPS = ((-1, -1, -1), (-1, -1, 0), (-1, 0, 0), (0, 0, 0), (0, 0, 1), (0, 1, 1), (1, 1, 1))
HOME = (-1, -1, 0, 0, 0, 1, 1)
FAR = -1e30
STEP = 4
ROWS = 16


def exchange(places, trunk_ref, side_ref, send_sem, recv_sem):
    row = lax.axis_index("diag")
    offset = lax.axis_index("off")
    shifts = [jnp.int32(-1), jnp.int32(1), offset - 1, offset, offset + 1]

    def inside(place):
        return (place >= 0) & (place < places)

    barrier = pltpu.get_barrier_semaphore()
    expected = jnp.int32(0)
    for slot, shift in enumerate(shifts):
        arrives = inside(row + shift) & (shift != 0)

        @pl.when(arrives)
        def _():
            pl.semaphore_signal(
                barrier, inc=1, device_id=(row + shift, offset), device_id_type=MESH
            )

        @pl.when(jnp.logical_not(inside(row + shift)))
        def _():
            side_ref[slot] = jnp.zeros_like(trunk_ref[...])

        @pl.when(shift == 0)
        def _():
            side_ref[slot] = trunk_ref[...]

        expected = expected + jnp.where(inside(row - shift) & (shift != 0), 1, 0)
    pl.semaphore_wait(barrier, expected)

    def copy(slot, target):
        return pltpu.make_async_remote_copy(
            src_ref=trunk_ref,
            dst_ref=side_ref.at[slot],
            send_sem=send_sem.at[slot],
            recv_sem=recv_sem.at[slot],
            device_id=(target, offset),
            device_id_type=MESH,
        )

    for slot, shift in enumerate(shifts):

        @pl.when(inside(row - shift) & (shift != 0))
        def _():
            copy(slot, row - shift).start()

    for slot, shift in enumerate(shifts):

        @pl.when(inside(row - shift) & (shift != 0))
        def _():
            copy(slot, row - shift).wait_send()

        @pl.when(inside(row + shift) & (shift != 0))
        def _():
            copy(slot, row + shift).wait_recv()


def pick(table, lanes):
    return jnp.take_along_axis(table, lanes, axis=1, mode="promise_in_bounds")


def column(row):
    size = row.shape[1]
    shape = (size, size)
    same = lax.broadcasted_iota(jnp.int32, shape, 0) == lax.broadcasted_iota(jnp.int32, shape, 1)
    return jnp.sum(jnp.where(same, row, 0.0), axis=1, keepdims=True)


def head(places, offsets, trunk_ref, side_ref, w1_ref, b1_ref, w2_ref, b2_ref, out_ref,
         rows_ref, cols_ref, one_ref, two_ref, acc_ref):
    channels, width = trunk_ref.shape
    hid = w1_ref.shape[2]
    row = lax.axis_index("diag")
    offset = lax.axis_index("off")
    line = 2 * width

    def in_band(up, across):
        gap = offset + across - up
        ok = (row + up >= 0) & (row + up < places)
        ok = ok & (row + offset + across >= 0) & (row + offset + across < places)
        return jnp.where(ok & (gap >= 0) & (gap < offsets), 1.0, 0.0).astype(jnp.float32)

    band = {(a, b): in_band(a, b) for a in (-1, 0, 1) for b in (-1, 0, 1)}
    at = lax.broadcasted_iota(jnp.int32, (1, line), 1)

    def by_place(shift, low, mid, high):
        return jnp.where(at < 4 - shift, low, jnp.where(at < 4 - shift + width, mid, high))

    def shifted(before, own, after):
        whole = jnp.concatenate([before, own, after], axis=1).astype(jnp.float32)
        return [
            whole[:, width - 6 + 2 * tap : width - 6 + 2 * tap + line].astype(jnp.bfloat16)
            for tap in range(3)
        ]

    blank = jnp.zeros((channels, line), jnp.bfloat16)
    row_x = shifted(side_ref[0], trunk_ref[...], side_ref[1])
    col_x = shifted(side_ref[2], side_ref[3], side_ref[4])
    row_terms, col_terms = {}, {}
    for tap in range(3):
        weights = jnp.concatenate([w1_ref[tap, v] for v in range(3)], axis=0)
        got = jnp.dot(weights, jnp.concatenate([row_x[tap], blank], axis=0),
                      preferred_element_type=jnp.float32)
        for v in range(3):
            row_terms[tap, v] = got[v * hid : (v + 1) * hid]
        weights = jnp.concatenate([w1_ref[u, tap] for u in range(3)], axis=0)
        got = jnp.dot(weights, jnp.concatenate([blank, col_x[tap]], axis=0),
                      preferred_element_type=jnp.float32)
        for u in range(3):
            col_terms[u, tap] = got[u * hid : (u + 1) * hid]

    row_sums, col_sums = {}, {}
    for side in (-1, 0, 1):
        row_keep = [by_place(2 * (t - 1), band[-1, side], band[0, side], band[1, side]) for t in range(3)]
        col_keep = [by_place(2 * (t - 1), band[side, -1], band[side, 0], band[side, 1]) for t in range(3)]
        for t in range(3):
            row_sums[t, side] = sum(row_keep[u] * row_terms[u, t] for u in range(3))
            col_sums[t, side] = sum(col_keep[v] * col_terms[t, v] for v in range(3))

    slot = lax.broadcasted_iota(jnp.int32, (hid, width), 1)
    blocks = rows_ref.shape[0]
    per = width // ROWS
    for block in range(blocks):
        start = (block // per) * width
        lanes = (block % per) * ROWS + slot % ROWS
        table = None
        for group in range(7):
            values = sum(row_sums[v, TAPS[group][v]][:, start : start + width] for v in range(3))
            values = pick(values, lanes)
            table = values if table is None else jnp.where(slot // ROWS == group, values, table)
        rows_ref[block] = table

    bias = column(b1_ref[...])
    for group in range(7):
        values = sum(col_sums[u, TAPS[group][u]] for u in range(3)) + bias
        kept = by_place(0, band[HOME[group], -1], band[HOME[group], 0], band[HOME[group], 1])
        values = jnp.where(kept > 0.5, values, FAR)
        for v in range(3):
            cols_ref[group, v * hid : (v + 1) * hid] = values[:, 4 * v : 4 * v + width]

    one_ref[...] = jnp.zeros_like(one_ref)
    two_ref[...] = jnp.zeros_like(two_ref)
    bias2 = column(b2_ref[...])

    def group_of(place):
        group = jnp.int32(0)
        for edge in (2, 4, 6, width + 2, width + 4, width + 6):
            group = group + jnp.where(place >= edge, 1, 0)
        return group

    picks = []
    for v in range(3):
        place = slot + 4 * v
        group = jnp.zeros_like(place)
        for edge in (2, 4, 6, width + 2, width + 4, width + 6):
            group = group + jnp.where(place >= edge, 1, 0)
        picks.append(group * ROWS)

    def chunk(base):
        columns = []
        for step in range(STEP):
            place = base + step
            table = rows_ref[place // ROWS]
            cols = cols_ref[group_of(place)]
            within = place % ROWS
            parts = [
                jnp.maximum(pick(table, picks[v] + within) + cols[v * hid : (v + 1) * hid], 0.0)
                for v in range(3)
            ]
            columns.append(jnp.concatenate(parts, axis=0).astype(jnp.bfloat16))
        got = jnp.dot(w2_ref[...], jnp.concatenate(columns, axis=1),
                      preferred_element_type=jnp.float32)
        done = two_ref[...] + got[2 * hid :] + bias2
        two_ref[...] = one_ref[...] + got[hid : 2 * hid]
        one_ref[...] = got[:hid]
        for step in range(STEP):
            acc_ref[pl.ds((base + step) * hid, hid)] = done[:, step * width : (step + 1) * width]

    chunk(jnp.int32(0))
    chunk(jnp.int32(STEP))

    @pl.loop(0, width // ROWS)
    def _(block):
        for step in range(ROWS // STEP):
            chunk(8 + block * ROWS + step * STEP)
        for h in range(hid):
            rows = acc_ref[pl.ds((8 + block * ROWS) * hid + h, ROWS, stride=hid), :]
            out_ref[h, pl.ds(pl.multiple_of(block * ROWS, ROWS), ROWS), :] = rows.astype(out_ref.dtype)


def local(places, offsets, trunk, w_first, b_first, w_second, b_second):
    channels, width = trunk.shape[2:]
    hid = w_first.shape[0]
    trunk = trunk.reshape(channels, width)
    vmem = pl.BlockSpec(memory_space=pltpu.VMEM)
    side = pl.pallas_call(
        functools.partial(exchange, places),
        out_shape=jax.ShapeDtypeStruct((5, channels, width), trunk.dtype),
        in_specs=[vmem],
        out_specs=vmem,
        scratch_shapes=[pltpu.SemaphoreType.DMA((5,)), pltpu.SemaphoreType.DMA((5,))],
        compiler_params=pltpu.CompilerParams(collective_id=0, has_side_effects=True),
        name="exchange",
    )(trunk)
    first = jnp.transpose(w_first, (2, 3, 0, 1))
    second = jnp.transpose(w_second, (2, 0, 3, 1)).reshape(3 * hid, 3 * hid)
    reach = width + 8
    result = pl.pallas_call(
        functools.partial(head, places, offsets),
        out_shape=jax.ShapeDtypeStruct((hid, width, width), jnp.bfloat16),
        in_specs=[vmem] * 6,
        out_specs=vmem,
        scratch_shapes=[
            pltpu.VMEM((pl.cdiv(reach, ROWS), hid, width), jnp.float32),
            pltpu.VMEM((7, 3 * hid, width), jnp.float32),
            pltpu.VMEM((hid, STEP * width), jnp.float32),
            pltpu.VMEM((hid, STEP * width), jnp.float32),
            pltpu.VMEM((reach * hid, width), jnp.float32),
        ],
        compiler_params=pltpu.CompilerParams(vmem_limit_bytes=32 * 1024 * 1024),
        name="head",
    )(trunk, side, first, b_first.reshape(1, hid), second, b_second.reshape(1, hid))
    return result[None, None, None]


def solution(mesh):
    placed = (P("diag", None, None, None), P(), P(), P(), P())
    return jax.shard_map(
        functools.partial(local, mesh.shape["diag"], mesh.shape["off"]),
        mesh=mesh,
        in_specs=placed,
        out_specs=P("diag", "off", None, None, None, None),
        check_vma=False,
    )
```

```python
import functools

import jax
import jax.numpy as jnp
from jax import lax
from jax.experimental import pallas as pl
from jax.experimental.pallas import tpu as pltpu
from jax.sharding import PartitionSpec as P

MESH = pl.DeviceIdType.MESH
TAPS = ((-1, -1, -1), (-1, -1, 0), (-1, 0, 0), (0, 0, 0), (0, 0, 1), (0, 1, 1), (1, 1, 1))
HOME = (-1, -1, 0, 0, 0, 1, 1)
VARIANTS = ((0, 2, 3), (1, 3, 3), (2, 3, 3), (3, 3, 3), (3, 3, 4), (3, 3, 5), (3, 4, 6))
FAR = -1e30
SIDES = (-1, 0, 1)
EDGE = 8
STEP = 4
ROWS = 16


def exchange(places, own_ref, first_ref, second_ref, bias1_ref, bias2_ref,
             side_ref, w1_ref, w2_ref, b1_ref, b2_ref,
             trunk_ref, raw_ref, load_sem, send_sem, recv_sem):
    hid = raw_ref.shape[2]
    loads = [
        pltpu.make_async_copy(source, target, load_sem.at[i])
        for i, (source, target) in enumerate((
            (own_ref, trunk_ref), (second_ref, raw_ref), (first_ref, w1_ref),
            (bias1_ref, b1_ref), (bias2_ref, b2_ref),
        ))
    ]
    for load in loads:
        load.start()
    row = lax.axis_index("diag")
    offset = lax.axis_index("off")
    shifts = [jnp.int32(-1), jnp.int32(1), offset - 1, offset, offset + 1]

    def inside(place):
        return (place >= 0) & (place < places)

    barrier = pltpu.get_barrier_semaphore()
    for shift in shifts:
        arrives = inside(row + shift) & (shift != 0)

        @pl.when(arrives)
        def _():
            pl.semaphore_signal(
                barrier, inc=1, device_id=(row + shift, offset), device_id_type=MESH
            )

    loads[0].wait()
    expected = jnp.int32(0)
    for slot, shift in enumerate(shifts):

        @pl.when(jnp.logical_not(inside(row + shift)))
        def _():
            side_ref[slot] = jnp.zeros(trunk_ref.shape, trunk_ref.dtype)

        @pl.when(shift == 0)
        def _():
            side_ref[slot] = trunk_ref[...]

        expected = expected + jnp.where(inside(row - shift) & (shift != 0), 1, 0)
    pl.semaphore_wait(barrier, expected)

    def copy(slot, target):
        return pltpu.make_async_remote_copy(
            src_ref=trunk_ref,
            dst_ref=side_ref.at[slot],
            send_sem=send_sem.at[slot],
            recv_sem=recv_sem.at[slot],
            device_id=(target, offset),
            device_id_type=MESH,
        )

    for slot, shift in enumerate(shifts):

        @pl.when(inside(row - shift) & (shift != 0))
        def _():
            copy(slot, row - shift).start()

    side_ref[5] = trunk_ref[...]
    loads[1].wait()
    for u in range(3):
        taps = [raw_ref[u, v].astype(jnp.float32) for v in range(3)]
        w2_ref[u * hid : (u + 1) * hid] = jnp.concatenate(taps, axis=1).astype(w2_ref.dtype)
    for load in loads[2:]:
        load.wait()

    for slot, shift in enumerate(shifts):

        @pl.when(inside(row - shift) & (shift != 0))
        def _():
            copy(slot, row - shift).wait_send()

        @pl.when(inside(row + shift) & (shift != 0))
        def _():
            copy(slot, row + shift).wait_recv()


def column(row):
    size = row.shape[1]
    shape = (size, size)
    same = lax.broadcasted_iota(jnp.int32, shape, 0) == lax.broadcasted_iota(jnp.int32, shape, 1)
    return jnp.sum(jnp.where(same, row, 0.0), axis=1, keepdims=True)


def outer(left, right):
    return lax.dot_general(left, right, (((1,), (1,)), ((), ())), preferred_element_type=jnp.float32)


def head(places, offsets, side_ref, w1_ref, w2_ref, b1_ref, b2_ref, out_ref,
         rows_ref, cols_ref, one_ref, two_ref, acc_ref, tile_ref, out_sem):
    channels, width = side_ref.shape[1:]
    hid = w1_ref.shape[2]
    row = lax.axis_index("diag")
    offset = lax.axis_index("off")
    reach = width + 8

    def in_band(up, across):
        gap = offset + across - up
        ok = (row + up >= 0) & (row + up < places)
        ok = ok & (row + offset + across >= 0) & (row + offset + across < places)
        return jnp.where(ok & (gap >= 0) & (gap < offsets), 1.0, 0.0).astype(jnp.float32)

    band = {(a, b): in_band(a, b) for a in SIDES for b in SIDES}

    def by_place(at, shift, low, mid, high):
        return jnp.where(at < 4 - shift, low, jnp.where(at < 4 - shift + width, mid, high))

    whole = jnp.concatenate([
        jnp.concatenate([side_ref[0], side_ref[5], side_ref[1]], axis=1),
        jnp.concatenate([side_ref[2], side_ref[3], side_ref[4]], axis=1),
    ], axis=0).astype(jnp.float32).T
    bins = [whole[width - 6 + 2 * t : width - 6 + 2 * t + reach] for t in range(3)]
    lane = lax.broadcasted_iota(jnp.int32, (reach, 2 * channels), 1)
    at = lax.broadcasted_iota(jnp.int32, (reach, 2 * channels), 0)
    row_sums, col_sums = {}, {}
    row_left, col_left = [], []
    for side in SIDES:
        row_left.append(jnp.concatenate([
            bins[t] * jnp.where(lane < channels, by_place(
                at, 2 * (t - 1), band[-1, side], band[0, side], band[1, side]), 0.0)
            for t in range(3)], axis=1))
        col_left.append(jnp.concatenate([
            bins[t] * jnp.where(lane >= channels, by_place(
                at, 2 * (t - 1), band[side, -1], band[side, 0], band[side, 1]), 0.0)
            for t in range(3)], axis=1))
    row_left = jnp.concatenate(row_left, axis=0).astype(jnp.bfloat16)
    col_left = jnp.concatenate(col_left, axis=0).astype(jnp.bfloat16)
    for t in range(3):
        row_taps = jnp.concatenate([w1_ref[u, t] for u in range(3)], axis=1)
        col_taps = jnp.concatenate([w1_ref[t, v] for v in range(3)], axis=1)
        row_got = outer(row_left, jnp.concatenate([row_taps] * 3, axis=0))
        col_got = outer(col_left, jnp.concatenate([col_taps] * 3, axis=0))
        for i, side in enumerate(SIDES):
            row_sums[t, side] = row_got[i * reach : (i + 1) * reach]
            col_sums[t, side] = col_got[i * reach : (i + 1) * reach]

    wide = lax.broadcasted_iota(jnp.int32, (reach, 3 * hid), 1)

    def by_tap(first, mid, last):
        shape = first.shape
        return jnp.where(wide[: shape[0]] < hid, first, jnp.where(wide[: shape[0]] < 2 * hid, mid, last))

    row_terms = [sum(row_sums[v, TAPS[group][v]] for v in range(3)) for group in range(7)]
    for i, groups in enumerate(VARIANTS):
        rows_ref[i] = by_tap(*[row_terms[group] for group in groups])

    bias = jnp.concatenate([b1_ref[...]] * 3, axis=1)
    place = lax.broadcasted_iota(jnp.int32, (reach, 3 * hid), 0)
    for group in range(7):
        values = sum(col_sums[u, TAPS[group][u]] for u in range(3)) + bias
        kept = by_place(place, 0, band[HOME[group], -1], band[HOME[group], 0], band[HOME[group], 1])
        values = jnp.where(kept > 0.5, values, FAR)
        cols_ref[group] = by_tap(*[values[4 * v : 4 * v + width] for v in range(3)])

    one_ref[...] = jnp.zeros_like(one_ref)
    two_ref[...] = jnp.zeros_like(two_ref)
    bias2 = column(b2_ref[...])
    pair = lax.broadcasted_iota(jnp.int32, (EDGE, 3 * hid), 0) // 2

    def group_of(place):
        group = jnp.int32(0)
        for edge in (2, 4, 6, width + 2, width + 4, width + 6):
            group = group + jnp.where(place >= edge, 1, 0)
        return group

    def chunk(base):
        cells = []
        for step in range(STEP):
            place = base + step
            cols = cols_ref.at[group_of(place)]
            term = [rows_ref[i, pl.ds(place, 1), :] for i in range(7)]
            low = jnp.where(pair == 0, term[0], jnp.where(pair == 1, term[1], jnp.where(pair == 2, term[2], term[3])))
            high = jnp.where(pair == 3, term[6], jnp.where(pair == 2, term[5], jnp.where(pair == 1, term[4], term[3])))
            cells.append(cols[:EDGE] + low)
            cells.append(cols[EDGE : width - EDGE] + term[3])
            cells.append(cols[width - EDGE :] + high)
        hidden = jnp.maximum(jnp.concatenate(cells, axis=0), 0.0).astype(jnp.bfloat16)
        got = outer(w2_ref[...], hidden)
        done = two_ref[...] + got[2 * hid :] + bias2
        two_ref[...] = one_ref[...] + got[hid : 2 * hid]
        one_ref[...] = got[:hid]
        for step in range(STEP):
            acc_ref[pl.ds((base + step) * hid, hid)] = done[:, step * width : (step + 1) * width]

    chunk(jnp.int32(0))
    chunk(jnp.int32(STEP))

    def store(block):
        part = pl.ds(pl.multiple_of(block * ROWS, ROWS), ROWS)
        return pltpu.make_async_copy(tile_ref.at[:, part, :], out_ref.at[:, part, :], out_sem.at[block])

    @pl.loop(0, width // ROWS)
    def _(block):
        for step in range(ROWS // STEP):
            chunk(8 + block * ROWS + step * STEP)
        for h in range(hid):
            rows = acc_ref[pl.ds((8 + block * ROWS) * hid + h, ROWS, stride=hid), :]
            tile_ref[h, pl.ds(pl.multiple_of(block * ROWS, ROWS), ROWS), :] = rows.astype(tile_ref.dtype)
        store(block).start()

    for block in range(width // ROWS):
        store(block).wait()


def local(places, offsets, trunk, w_first, b_first, w_second, b_second):
    channels, width = trunk.shape[2:]
    hid = w_first.shape[0]
    trunk = trunk.reshape(channels, width)
    first = jnp.transpose(w_first, (2, 3, 0, 1))
    second = jnp.transpose(w_second, (2, 3, 0, 1))
    vmem = pl.BlockSpec(memory_space=pltpu.VMEM)
    hbm = pl.BlockSpec(memory_space=pltpu.HBM)
    limit = 40 * 1024 * 1024
    staged = pl.pallas_call(
        functools.partial(exchange, places),
        out_shape=(
            pltpu.VMEM((6, channels, width), trunk.dtype),
            pltpu.VMEM(first.shape, first.dtype),
            pltpu.VMEM((3 * hid, 3 * hid), second.dtype),
            pltpu.VMEM((1, hid), b_first.dtype),
            pltpu.VMEM((1, hid), b_second.dtype),
        ),
        in_specs=[hbm] * 5,
        out_specs=(vmem,) * 5,
        scratch_shapes=[
            pltpu.VMEM((channels, width), trunk.dtype),
            pltpu.VMEM(second.shape, second.dtype),
            pltpu.SemaphoreType.DMA((5,)),
            pltpu.SemaphoreType.DMA((5,)),
            pltpu.SemaphoreType.DMA((5,)),
        ],
        compiler_params=pltpu.CompilerParams(
            collective_id=0, has_side_effects=True, vmem_limit_bytes=limit
        ),
        name="exchange",
    )(*[pltpu.with_memory_space_constraint(a, pltpu.HBM) for a in (
        trunk, first, second, b_first.reshape(1, hid), b_second.reshape(1, hid))])
    reach = width + 8
    result = pl.pallas_call(
        functools.partial(head, places, offsets),
        out_shape=jax.ShapeDtypeStruct((hid, width, width), jnp.bfloat16),
        in_specs=[vmem] * 5,
        out_specs=hbm,
        scratch_shapes=[
            pltpu.VMEM((7, reach, 3 * hid), jnp.float32),
            pltpu.VMEM((7, width, 3 * hid), jnp.float32),
            pltpu.VMEM((hid, STEP * width), jnp.float32),
            pltpu.VMEM((hid, STEP * width), jnp.float32),
            pltpu.VMEM((reach * hid, width), jnp.float32),
            pltpu.VMEM((hid, width, width), jnp.bfloat16),
            pltpu.SemaphoreType.DMA((width // ROWS,)),
        ],
        compiler_params=pltpu.CompilerParams(vmem_limit_bytes=limit),
        name="head",
    )(*staged)
    return result[None, None, None]


def solution(mesh):
    placed = (P("diag", None, None, None), P(), P(), P(), P())
    return jax.shard_map(
        functools.partial(local, mesh.shape["diag"], mesh.shape["off"]),
        mesh=mesh,
        in_specs=placed,
        out_specs=P("diag", "off", None, None, None, None),
        check_vma=False,
    )
```

```python
import functools

import jax
import jax.numpy as jnp
from jax import lax
from jax.experimental import pallas as pl
from jax.experimental.pallas import tpu as pltpu
from jax.sharding import PartitionSpec as P

MESH = pl.DeviceIdType.MESH
TAPS = ((-1, -1, -1), (-1, -1, 0), (-1, 0, 0), (0, 0, 0), (0, 0, 1), (0, 1, 1), (1, 1, 1))
HOME = (-1, -1, 0, 0, 0, 1, 1)
VARIANTS = ((0, 2, 3), (1, 3, 3), (2, 3, 3), (3, 3, 3), (3, 3, 4), (3, 3, 5), (3, 4, 6))
FAR = -1e30
SIDES = (-1, 0, 1)
EDGE = 8
STEP = 4
ROWS = 16


def exchange(places, own_ref, first_ref, second_ref, bias1_ref, bias2_ref,
             side_ref, w1_ref, w2_ref, b1_ref, b2_ref,
             trunk_ref, raw_ref, load_sem, send_sem, recv_sem):
    row = lax.axis_index("diag")
    offset = lax.axis_index("off")
    shifts = [jnp.int32(-1), jnp.int32(1), offset - 1, offset, offset + 1]

    def inside(place):
        return (place >= 0) & (place < places)

    barrier = pltpu.get_barrier_semaphore()
    for shift in shifts:
        arrives = inside(row + shift) & (shift != 0)

        @pl.when(arrives)
        def _():
            pl.semaphore_signal(
                barrier, inc=1, device_id=(row + shift, offset), device_id_type=MESH
            )

    hid = raw_ref.shape[2]
    loads = [
        pltpu.make_async_copy(source, target, load_sem.at[i])
        for i, (source, target) in enumerate((
            (own_ref, trunk_ref), (second_ref, raw_ref), (first_ref, w1_ref),
            (bias1_ref, b1_ref), (bias2_ref, b2_ref),
        ))
    ]
    for load in loads:
        load.start()
    loads[0].wait()
    expected = jnp.int32(0)
    for shift in shifts:
        expected = expected + jnp.where(inside(row - shift) & (shift != 0), 1, 0)
    pl.semaphore_wait(barrier, expected)

    def copy(slot, target):
        return pltpu.make_async_remote_copy(
            src_ref=trunk_ref,
            dst_ref=side_ref.at[slot],
            send_sem=send_sem.at[slot],
            recv_sem=recv_sem.at[slot],
            device_id=(target, offset),
            device_id_type=MESH,
        )

    for slot, shift in enumerate(shifts):

        @pl.when(inside(row - shift) & (shift != 0))
        def _():
            copy(slot, row - shift).start()

    side_ref[5] = trunk_ref[...]
    for slot, shift in enumerate(shifts):

        @pl.when(jnp.logical_not(inside(row + shift)))
        def _():
            side_ref[slot] = jnp.zeros(trunk_ref.shape, trunk_ref.dtype)

        @pl.when(shift == 0)
        def _():
            side_ref[slot] = trunk_ref[...]

    loads[1].wait()
    for u in range(3):
        taps = [raw_ref[u, v].astype(jnp.float32) for v in range(3)]
        w2_ref[u * hid : (u + 1) * hid] = jnp.concatenate(taps, axis=1).astype(w2_ref.dtype)
    for load in loads[2:]:
        load.wait()

    for slot, shift in enumerate(shifts):

        @pl.when(inside(row - shift) & (shift != 0))
        def _():
            copy(slot, row - shift).wait_send()

        @pl.when(inside(row + shift) & (shift != 0))
        def _():
            copy(slot, row + shift).wait_recv()


def column(row):
    size = row.shape[1]
    shape = (size, size)
    same = lax.broadcasted_iota(jnp.int32, shape, 0) == lax.broadcasted_iota(jnp.int32, shape, 1)
    return jnp.sum(jnp.where(same, row, 0.0), axis=1, keepdims=True)


def outer(left, right):
    return lax.dot_general(left, right, (((1,), (1,)), ((), ())), preferred_element_type=jnp.float32)


def head(places, offsets, side_ref, w1_ref, w2_ref, b1_ref, b2_ref, out_ref,
         rows_ref, cols_ref, one_ref, two_ref, acc_ref, tile_ref, out_sem):
    channels, width = side_ref.shape[1:]
    hid = w1_ref.shape[2]
    row = lax.axis_index("diag")
    offset = lax.axis_index("off")
    reach = width + 8

    def in_band(up, across):
        gap = offset + across - up
        ok = (row + up >= 0) & (row + up < places)
        ok = ok & (row + offset + across >= 0) & (row + offset + across < places)
        return jnp.where(ok & (gap >= 0) & (gap < offsets), 1.0, 0.0).astype(jnp.float32)

    band = {(a, b): in_band(a, b) for a in SIDES for b in SIDES}

    def by_place(at, shift, low, mid, high):
        return jnp.where(at < 4 - shift, low, jnp.where(at < 4 - shift + width, mid, high))

    whole = jnp.concatenate([
        jnp.concatenate([side_ref[0], side_ref[5], side_ref[1]], axis=1),
        jnp.concatenate([side_ref[2], side_ref[3], side_ref[4]], axis=1),
    ], axis=0).astype(jnp.float32).T
    bins = [whole[width - 6 + 2 * t : width - 6 + 2 * t + reach] for t in range(3)]
    at = lax.broadcasted_iota(jnp.int32, (EDGE, 2 * channels), 0)

    def scaled(values, shift, low, mid, high):
        start = reach - EDGE
        return jnp.concatenate([
            values[:EDGE] * by_place(at, shift, low, mid, high),
            values[EDGE:start] * mid,
            values[start:] * by_place(at + start, shift, low, mid, high),
        ], axis=0)

    row_sums, col_sums = {}, {}
    row_left, col_left = [], []
    for side in SIDES:
        row_left.append(jnp.concatenate([
            scaled(bins[t], 2 * (t - 1), band[-1, side], band[0, side], band[1, side])
            for t in range(3)], axis=1))
        col_left.append(jnp.concatenate([
            scaled(bins[t], 2 * (t - 1), band[side, -1], band[side, 0], band[side, 1])
            for t in range(3)], axis=1))
    row_left = jnp.concatenate(row_left, axis=0).astype(jnp.bfloat16)
    col_left = jnp.concatenate(col_left, axis=0).astype(jnp.bfloat16)
    lane = lax.broadcasted_iota(jnp.int32, (hid, 2 * channels), 1)
    none = jnp.zeros((hid, 2 * channels), w1_ref.dtype)
    for t in range(3):
        row_taps = jnp.concatenate([jnp.where(lane < channels, w1_ref[u, t], none) for u in range(3)], axis=1)
        col_taps = jnp.concatenate([jnp.where(lane < channels, none, w1_ref[t, v]) for v in range(3)], axis=1)
        row_got = outer(row_left, jnp.concatenate([row_taps] * 3, axis=0))
        col_got = outer(col_left, jnp.concatenate([col_taps] * 3, axis=0))
        for i, side in enumerate(SIDES):
            row_sums[t, side] = row_got[i * reach : (i + 1) * reach]
            col_sums[t, side] = col_got[i * reach : (i + 1) * reach]

    wide = lax.broadcasted_iota(jnp.int32, (reach, 3 * hid), 1)

    def by_tap(first, mid, last):
        shape = first.shape
        return jnp.where(wide[: shape[0]] < hid, first, jnp.where(wide[: shape[0]] < 2 * hid, mid, last))

    row_terms = [sum(row_sums[v, TAPS[group][v]] for v in range(3)) for group in range(7)]
    for i, groups in enumerate(VARIANTS):
        rows_ref[i] = by_tap(*[row_terms[group] for group in groups])

    bias = jnp.concatenate([b1_ref[...]] * 3, axis=1)
    place = lax.broadcasted_iota(jnp.int32, (reach, 3 * hid), 0)
    for group in range(7):
        values = sum(col_sums[u, TAPS[group][u]] for u in range(3)) + bias
        kept = by_place(place, 0, band[HOME[group], -1], band[HOME[group], 0], band[HOME[group], 1])
        values = jnp.where(kept > 0.5, values, FAR)
        cols_ref[group] = by_tap(*[values[4 * v : 4 * v + width] for v in range(3)])

    one_ref[...] = jnp.zeros_like(one_ref)
    two_ref[...] = jnp.zeros_like(two_ref)
    bias2 = column(b2_ref[...])
    pair = lax.broadcasted_iota(jnp.int32, (EDGE, 3 * hid), 0) // 2

    def group_of(place):
        group = jnp.int32(0)
        for edge in (2, 4, 6, width + 2, width + 4, width + 6):
            group = group + jnp.where(place >= edge, 1, 0)
        return group

    def chunk(base):
        cells = []
        for step in range(STEP):
            place = base + step
            cols = cols_ref.at[group_of(place)]
            term = [rows_ref[i, pl.ds(place, 1), :] for i in range(7)]
            low = jnp.where(pair == 0, term[0], jnp.where(pair == 1, term[1], jnp.where(pair == 2, term[2], term[3])))
            high = jnp.where(pair == 3, term[6], jnp.where(pair == 2, term[5], jnp.where(pair == 1, term[4], term[3])))
            cells.append(cols[:EDGE] + low)
            cells.append(cols[EDGE : width - EDGE] + term[3])
            cells.append(cols[width - EDGE :] + high)
        hidden = jnp.maximum(jnp.concatenate(cells, axis=0).astype(jnp.bfloat16), jnp.bfloat16(0))
        got = outer(w2_ref[...], hidden)
        done = two_ref[...] + got[2 * hid :] + bias2
        two_ref[...] = one_ref[...] + got[hid : 2 * hid]
        one_ref[...] = got[:hid]
        for step in range(STEP):
            acc_ref[pl.ds((base + step) * hid, hid)] = done[:, step * width : (step + 1) * width]

    chunk(jnp.int32(0))
    chunk(jnp.int32(STEP))

    def store(block):
        part = pl.ds(pl.multiple_of(block * ROWS, ROWS), ROWS)
        return pltpu.make_async_copy(tile_ref.at[:, part, :], out_ref.at[:, part, :], out_sem.at[block])

    def chunks(block):
        for step in range(ROWS // STEP):
            chunk(8 + block * ROWS + step * STEP)

    def release(block):
        part = pl.ds(pl.multiple_of(block * ROWS, ROWS), ROWS)
        for h in range(hid):
            rows = acc_ref[pl.ds((8 + block * ROWS) * hid + h, ROWS, stride=hid), :]
            tile_ref[h, part, :] = rows.astype(tile_ref.dtype)
        store(block).start()

    blocks = width // ROWS
    chunks(jnp.int32(0))

    @pl.loop(1, blocks)
    def _(block):
        release(block - 1)
        chunks(block)

    release(jnp.int32(blocks - 1))
    for block in range(width // ROWS):
        store(block).wait()


def local(places, offsets, trunk, w_first, b_first, w_second, b_second):
    channels, width = trunk.shape[2:]
    hid = w_first.shape[0]
    trunk = trunk.reshape(channels, width)
    first = jnp.transpose(w_first, (2, 3, 0, 1))
    second = jnp.transpose(w_second, (2, 3, 0, 1))
    vmem = pl.BlockSpec(memory_space=pltpu.VMEM)
    hbm = pl.BlockSpec(memory_space=pltpu.HBM)
    limit = 40 * 1024 * 1024
    staged = pl.pallas_call(
        functools.partial(exchange, places),
        out_shape=(
            pltpu.VMEM((6, channels, width), trunk.dtype),
            pltpu.VMEM(first.shape, first.dtype),
            pltpu.VMEM((3 * hid, 3 * hid), second.dtype),
            pltpu.VMEM((1, hid), b_first.dtype),
            pltpu.VMEM((1, hid), b_second.dtype),
        ),
        in_specs=[hbm] * 5,
        out_specs=(vmem,) * 5,
        scratch_shapes=[
            pltpu.VMEM((channels, width), trunk.dtype),
            pltpu.VMEM(second.shape, second.dtype),
            pltpu.SemaphoreType.DMA((5,)),
            pltpu.SemaphoreType.DMA((5,)),
            pltpu.SemaphoreType.DMA((5,)),
        ],
        compiler_params=pltpu.CompilerParams(
            collective_id=0, has_side_effects=True, vmem_limit_bytes=limit
        ),
        name="exchange",
    )(*[pltpu.with_memory_space_constraint(a, pltpu.HBM) for a in (
        trunk, first, second, b_first.reshape(1, hid), b_second.reshape(1, hid))])
    reach = width + 8
    result = pl.pallas_call(
        functools.partial(head, places, offsets),
        out_shape=jax.ShapeDtypeStruct((hid, width, width), jnp.bfloat16),
        in_specs=[vmem] * 5,
        out_specs=hbm,
        scratch_shapes=[
            pltpu.VMEM((7, reach, 3 * hid), jnp.float32),
            pltpu.VMEM((7, width, 3 * hid), jnp.float32),
            pltpu.VMEM((hid, STEP * width), jnp.float32),
            pltpu.VMEM((hid, STEP * width), jnp.float32),
            pltpu.VMEM((reach * hid, width), jnp.float32),
            pltpu.VMEM((hid, width, width), jnp.bfloat16),
            pltpu.SemaphoreType.DMA((width // ROWS,)),
        ],
        compiler_params=pltpu.CompilerParams(vmem_limit_bytes=limit),
        name="head",
    )(*staged)
    return result[None, None, None]


def solution(mesh):
    placed = (P("diag", None, None, None), P(), P(), P(), P())
    return jax.shard_map(
        functools.partial(local, mesh.shape["diag"], mesh.shape["off"]),
        mesh=mesh,
        in_specs=placed,
        out_specs=P("diag", "off", None, None, None, None),
        check_vma=False,
    )
```
